32 devices in a mesh: ctx: 16 (over z, y, core), tp: 2 (over x).
Axes of the slice: x: 2, y: 2, z: 4, core: 2. Of those that a mesh axis runs over, the one named last changes fastest.
Arguments:
- attended: bfloat16 [4096, 4096], P('ctx', 'tp'), may hold values from -6 to 6
- out_proj: bfloat16 [4096, 4096], P('tp'), may hold values from -0.09375 to 0.09375
- residual: bfloat16 [4096, 4096], P(('ctx', 'tp')), may hold values from -6 to 6
- norm_gain: float32 [4096], replicated, may hold values from 0.5 to 1.5
- cond_proj: bfloat16 [4096, 2048], P(None, 'tp'), may hold values from -0.09375 to 0.09375
- noise_proj: bfloat16 [128, 2048], P(None, 'tp'), may hold values from -0.5 to 0.5
- latent_proj: bfloat16 [2048, 128], P('tp'), may hold values from -0.176776695 to 0.176776695
- noise_draws: bfloat16 [4096, 8, 128], P('ctx'), may hold values from -6 to 6
- targets: bfloat16 [4096, 128], P(('ctx', 'tp')), may hold values from -9 to 9
Outputs:
- energies: float32 [4096], P(('ctx', 'tp'))
- cond_grad: bfloat16 [4096, 2048], P(None, 'tp')
- noise_grad: bfloat16 [128, 2048], P(None, 'tp')
- latent_grad: bfloat16 [2048, 128], P('tp')
The draws below stay inside these ranges and needn't reach their ends.
All inputs are finite; a program needn't handle non-finite values.
Results may differ from the reference program's by a relative error of at most 0.018.
Values may be sent and summed in bfloat16 or wider, within the bound.
A program may use at most 128 MiB of HBM per device.

```python
import math
import jax
import jax.numpy as jnp
from jax import lax

D = 4096
HW = 2048
LAT = 128
NZ = 128
S = 8
POS = 4096
N_TP = 2


def draw_latent_proj(key, part):
    key = jax.random.fold_in(key, 11)
    position = jnp.arange(HW, dtype=jnp.float32)[:, None] / HW
    values = jax.random.truncated_normal(key, -4.0, 4.0, (HW, LAT), jnp.float32)
    scales = 0.5 * jnp.exp(position * 1.3862944)
    return (values * scales / HW ** 0.5).astype(jnp.bfloat16)


def levels(key, dims, cuts, least, high):
    gain, own = 1.0, jax.random.fold_in(key, 6)
    for axis_at, blocks in cuts:
        heights = jnp.exp(jax.random.uniform(jax.random.fold_in(own, axis_at), (blocks,), jnp.float32, least / len(cuts), high / len(cuts)))
        gain = gain * jnp.repeat(heights, dims[axis_at] // blocks).reshape([-1 if axis == axis_at else 1 for axis in range(len(dims))])
    return gain


def centred(stream_key, dims, width, bound, cuts=(), held_as=jnp.bfloat16):
    array = width * jax.random.normal(stream_key, dims, jnp.float32)
    if cuts:
        array = array * levels(stream_key, dims, cuts, -0.22, 0.18)
    return jnp.clip(array, -bound, bound).astype(held_as)


def setup_inputs(seed: int = 0) -> dict:
    keys = jax.random.split(jax.random.key(seed), 10)
    return {
        "attended": centred(keys[0], (POS, D), 1.0, 6.0, ((0, 16), (1, 2))),
        "out_proj": centred(keys[1], (D, D), D ** -0.5, 0.09375, ((0, 2),)),
        "residual": centred(keys[2], (POS, D), 1.0, 6.0, ((0, 32),)),
        "norm_gain": jnp.clip(1.0 + 0.1 * jax.random.normal(keys[3], (D,), jnp.float32), 0.5, 1.5),
        "cond_proj": centred(keys[4], (D, HW), D ** -0.5, 0.09375, ((1, 2),)),
        "noise_proj": centred(keys[5], (NZ, HW), NZ ** -0.5, 0.5, ((1, 2),)),
        "latent_proj": draw_latent_proj(jax.random.fold_in(keys[9], 71), 0),
        "noise_draws": centred(keys[7], (POS, S, NZ), 1.0, 6.0, ((0, 16),)),
        "targets": centred(keys[8], (POS, LAT), 1.5, 9.0, ((0, 32),)),
    }


def silu_slope(values):
    sigmoid = jax.nn.sigmoid(values)
    return sigmoid * (1.0 + values * (1.0 - sigmoid))

def energy_score(samples, goal_rows):
    n_draws = samples.shape[1]
    diff_t = samples - goal_rows[:, None, :]
    dist_t = jnp.sqrt(lax.optimization_barrier(jnp.sum(diff_t * diff_t, axis=-1)) + 1.0)
    diff_p = samples[:, :, None, :] - samples[:, None, :, :]
    dist_p = jnp.sqrt(lax.optimization_barrier(jnp.sum(diff_p * diff_p, axis=-1)) + 1.0)
    off_diag = 1.0 - jnp.eye(n_draws, dtype=jnp.float32)
    pair_count = n_draws * (n_draws - 1)
    energies = lax.optimization_barrier(jnp.mean(dist_t, axis=1)) - lax.optimization_barrier(jnp.sum(dist_p * off_diag, axis=(1, 2))) / (2.0 * pair_count)
    slopes = diff_t / (n_draws * dist_t[..., None]) - lax.optimization_barrier(jnp.sum(diff_p / dist_p[..., None], axis=2)) / pair_count
    return (energies, slopes.astype(jnp.bfloat16))

def widen(values):
    return lax.optimization_barrier(values).astype(jnp.float32)

def reference(attended, out_proj, residual, norm_gain, cond_proj, noise_proj, latent_proj, noise_draws, targets):
    group_width = D // N_TP
    summed = jnp.zeros((POS, D), jnp.float32)
    for group in range(N_TP):
        lower = group * group_width
        upper = lower + group_width
        partial_value = jnp.dot(attended[:, lower:upper], out_proj[lower:upper], preferred_element_type=jnp.float32).astype(jnp.bfloat16)
        summed = summed + widen(partial_value)
    hidden = residual.astype(jnp.float32) + summed
    normed = (hidden * lax.rsqrt(lax.optimization_barrier(jnp.mean(hidden * hidden, axis=-1, keepdims=True)) + 1e-05) * norm_gain).astype(jnp.bfloat16)
    block_rows = math.gcd(POS, 1024)
    blocks = POS // block_rows
    inputs = (normed.reshape(blocks, block_rows, D), noise_draws.reshape(blocks, block_rows, S, NZ), targets.reshape(blocks, block_rows, LAT))
    cond_w = cond_proj
    noise_w = noise_proj.astype(jnp.float32)
    latent_w = latent_proj.astype(jnp.float32)

    def head_block(grads, pieces):
        rows_normed, rows_noise, rows_goal = pieces
        condition = jnp.dot(rows_normed, cond_w, preferred_element_type=jnp.float32)
        preact = condition[:, None, :] + jnp.einsum('rsn,nh->rsh', rows_noise.astype(jnp.float32), noise_w)
        activation = jax.nn.silu(preact).astype(jnp.bfloat16)
        act_wide = widen(activation)
        samples = jnp.einsum('rsh,hl->rsl', act_wide, latent_w)
        energies, slopes = energy_score(samples, rows_goal.astype(jnp.float32))
        slope_wide = widen(slopes)
        latent_part = jnp.einsum('rsh,rsl->hl', act_wide, slope_wide)
        backward = jnp.einsum('rsl,hl->rsh', slope_wide, latent_w)
        pre_grad = (backward * silu_slope(preact)).astype(jnp.bfloat16)
        pre_wide = widen(pre_grad)
        noise_part = jnp.einsum('rsn,rsh->nh', rows_noise.astype(jnp.float32), pre_wide)
        cond_slope = lax.optimization_barrier(jnp.sum(pre_wide, axis=1)).astype(jnp.bfloat16)
        cond_part = jnp.dot(rows_normed.T, cond_slope, preferred_element_type=jnp.float32)
        return ((grads[0] + cond_part, grads[1] + noise_part, grads[2] + latent_part), energies)
    start_grads = (jnp.zeros((D, HW), jnp.float32), jnp.zeros((NZ, HW), jnp.float32), jnp.zeros((HW, LAT), jnp.float32))
    (cond_sum, noise_sum, latent_sum), energies = lax.scan(head_block, start_grads, inputs)
    squares_total = jnp.sum(cond_sum * cond_sum) + jnp.sum(noise_sum * noise_sum) + jnp.sum(latent_sum * latent_sum)
    rescale = lax.rsqrt(squares_total / (D * HW + NZ * HW + HW * LAT) + 1e-06)
    return (energies.reshape(POS), (cond_sum * rescale).astype(jnp.bfloat16), (noise_sum * rescale).astype(jnp.bfloat16), (latent_sum * rescale).astype(jnp.bfloat16))
```

```python
import functools

import jax
import jax.numpy as jnp
from jax import lax
from jax.experimental import pallas as pl
from jax.experimental.pallas import tpu as pltpu
from jax.sharding import PartitionSpec as P

ROWS = 64
BLOCK = 256
QUADS = 4
MESH = pl.DeviceIdType.MESH

D = 4096
HW = 2048
LAT = 128
NZ = 128


def silu_slope(values):
    sigmoid = jax.nn.sigmoid(values)
    return sigmoid * (1.0 + values * (1.0 - sigmoid))


def energy_score(samples, goal_rows):
    n_draws = samples.shape[1]
    diff_t = samples - goal_rows[:, None, :]
    dist_t = jnp.sqrt(jnp.sum(diff_t * diff_t, axis=-1) + 1.0)
    diff_p = samples[:, :, None, :] - samples[:, None, :, :]
    dist_p = jnp.sqrt(jnp.sum(diff_p * diff_p, axis=-1) + 1.0)
    off_diag = 1.0 - jnp.eye(n_draws, dtype=jnp.float32)
    pair_count = n_draws * (n_draws - 1)
    energies = jnp.mean(dist_t, axis=1) - jnp.sum(dist_p * off_diag, axis=(1, 2)) / (
        2.0 * pair_count
    )
    slopes = (
        diff_t / (n_draws * dist_t[..., None])
        - jnp.sum(diff_p / dist_p[..., None], axis=2) / pair_count
    )
    return (energies, slopes.astype(jnp.bfloat16))


def row_contract(left, right):
    return lax.dot_general(
        left, right, (((0,), (0,)), ((), ())), preferred_element_type=jnp.float32
    )


def grad_kernel(
    n_ctx,
    n_tp,
    scale_count,
    rows_ref,
    slope_ref,
    small_ref,
    out_ref,
    rescale_ref,
    slopes,
    smalls,
    prod,
    up,
    landed,
    squares,
    tp_squares,
    slope_send,
    slope_recv,
    small_send,
    small_recv,
    up_send,
    up_recv,
    down_send,
    down_recv,
    side_send,
    side_recv,
    core_send,
    core_recv,
    tp_send,
    tp_recv,
):
    chunks = prod.shape[0]
    grad_chunks = chunks - 1
    line = n_ctx // QUADS
    width = prod.shape[2]
    me = lax.axis_index("ctx")
    tp = lax.axis_index("tp")
    quad = lax.rem(me, QUADS)
    place = me // QUADS
    left = place < line // 2
    depth = jnp.where(left, place, line - 1 - place)
    middle = depth == line // 2 - 1
    inward = jnp.where(left, me + QUADS, me - QUADS)
    outward = jnp.where(left, me - QUADS, me + QUADS)
    mates = [None] + [
        (me - quad) + (quad + m - 2 * ((quad // m) % 2) * m if m < 3 else 3 - quad) for m in (1, 2, 3)
    ]
    mate_quads = [quad] + [mates[m] - (me - quad) for m in (1, 2, 3)]
    core, side = mates[1], mates[2]

    def remote(src, dst, send, recv, target, target_tp=None):
        return pltpu.make_async_remote_copy(
            src_ref=src,
            dst_ref=dst,
            send_sem=send,
            recv_sem=recv,
            device_id=(target, tp if target_tp is None else target_tp),
            device_id_type=MESH,
        )

    barrier = pltpu.get_barrier_semaphore()
    for mate in mates[1:]:
        pl.semaphore_signal(barrier, inc=1, device_id=(mate, tp), device_id_type=MESH)
    pl.semaphore_signal(barrier, inc=1, device_id=(inward, tp), device_id_type=MESH)

    @pl.when(depth > 0)
    def _():
        pl.semaphore_signal(barrier, inc=1, device_id=(outward, tp), device_id_type=MESH)

    for step in range(1, n_tp):
        pl.semaphore_signal(
            barrier, inc=1, device_id=(me, lax.rem(tp + step, n_tp)), device_id_type=MESH
        )
    pl.semaphore_wait(barrier, 4 + n_tp - 1 + jnp.where(depth > 0, 1, 0))

    slope_side = remote(slope_ref, slopes.at[1], slope_send.at[1], slope_recv.at[1], side)
    slope_core = remote(slope_ref, slopes.at[0], slope_send.at[0], slope_recv.at[0], core)
    slope_on = remote(slopes.at[1], slopes.at[2], slope_send.at[2], slope_recv.at[2], core)
    slope_side.start()
    slope_core.start()
    small_copies = [
        remote(
            small_ref.at[mate_quads[m]],
            smalls.at[m - 1],
            small_send.at[m - 1],
            small_recv.at[m - 1],
            mates[m],
        )
        for m in (1, 2, 3)
    ]
    for copy in small_copies:
        copy.start()

    squares[...] = jnp.zeros_like(squares)
    per_block = BLOCK // ROWS
    blocks = grad_chunks // per_block

    def product(m, block):
        columns = pl.ds(pl.multiple_of(block * BLOCK, BLOCK), BLOCK)
        right = slope_ref[...] if m == 0 else slopes[m - 1]
        return row_contract(rows_ref[m, :, columns], right).reshape(per_block, ROWS, width)

    def block_chunks(block):
        return pl.ds(block * per_block, per_block)

    def first_term(block, carry):
        prod[block_chunks(block)] = product(0, block)
        return carry

    def later_term(m):
        def term(block, carry):
            prod[block_chunks(block)] += product(m, block)
            return carry

        return term

    lax.fori_loop(0, blocks, first_term, 0)
    slope_core.wait_recv()
    lax.fori_loop(0, blocks, later_term(1), 0)
    slope_side.wait_recv()
    slope_on.start()
    lax.fori_loop(0, blocks, later_term(2), 0)
    slope_on.wait_recv()

    toward = jnp.where(middle, 1, 0)

    def up_copy(i):
        return remote(up.at[i], landed.at[toward, i], up_send.at[i], up_recv.at[toward, i], inward)

    def landed_wait(slot, i):
        remote(up.at[i], landed.at[slot, i], up_send.at[i], up_recv.at[slot, i], inward).wait_recv()

    def down_copy(i):
        return remote(
            out_ref.at[quad, i], out_ref.at[quad, i], down_send.at[i], down_recv.at[i], outward
        )

    def down_arrival(i):
        return remote(
            out_ref.at[quad, i], out_ref.at[quad, i], down_send.at[i], down_recv.at[i], inward
        )

    def side_copy(i):
        return remote(
            out_ref.at[quad, i], out_ref.at[quad, i], side_send.at[i], side_recv.at[i], side
        )

    def core_copy(slot, i):
        rows = out_ref.at[mate_quads[2 * slot], i]
        return remote(rows, rows, core_send.at[slot, i], core_recv.at[slot, i], core)

    def add_squares(which, i):
        wide = out_ref[which, i].astype(jnp.float32)
        squares[which] += jnp.sum((wide * wide).reshape(ROWS // 8, 8, width), axis=0)

    def go_up(i):
        @pl.when((i < grad_chunks) & (lax.rem(i, per_block) == 0))
        def _():
            block = i // per_block
            prod[block_chunks(block)] += product(3, block)

        @pl.when(i == grad_chunks)
        def _():
            total = small_ref[quad].astype(jnp.float32)
            for m, copy in enumerate(small_copies):
                copy.wait_recv()
                total = total + smalls[m].astype(jnp.float32)
            prod[grad_chunks] = total

        @pl.when(depth > 0)
        def _():
            landed_wait(0, i)
            up[i] = (prod[i] + landed[0, i].astype(jnp.float32)).astype(jnp.bfloat16)

        @pl.when(depth == 0)
        def _():
            up[i] = prod[i].astype(jnp.bfloat16)

        up_copy(i).start()

    def go_down(i):
        @pl.when(middle)
        def _():
            landed_wait(1, i)
            out_ref[quad, i] = (
                up[i].astype(jnp.float32) + landed[1, i].astype(jnp.float32)
            ).astype(jnp.bfloat16)

        @pl.when(jnp.logical_not(middle))
        def _():
            down_arrival(i).wait_recv()

        @pl.when(depth > 0)
        def _():
            down_copy(i).start()

        side_copy(i).start()
        core_copy(0, i).start()
        add_squares(quad, i)

    def hand_on(i):
        side_copy(i).wait_recv()
        core_copy(1, i).start()
        add_squares(mate_quads[2], i)

    def take_in(i):
        core_copy(0, i).wait_recv()
        core_copy(1, i).wait_recv()
        add_squares(mate_quads[1], i)
        add_squares(mate_quads[3], i)

    lag = 1 + 5 * (line // 2 - 1 - depth)
    longest = 1 + 5 * (line // 2 - 1)

    def step(t, carry):
        for behind, action in ((0, go_up), (lag, go_down), (lag + 2, hand_on), (lag + 3, take_in)):
            i = t - behind

            @pl.when((i >= 0) & (i < chunks))
            def _(i=i, action=action):
                action(i)

        return carry

    lax.fori_loop(0, chunks + longest + 3, step, 0)

    total = squares[0] + squares[1] + squares[2] + squares[3]
    folded = total[:, :128]
    for column in range(128, width, 128):
        folded = folded + total[:, column : column + 128]
    tp_squares[tp] = folded
    tp_copies = [
        remote(
            tp_squares.at[tp],
            tp_squares.at[tp],
            tp_send.at[shift - 1],
            tp_recv.at[shift - 1],
            me,
            lax.rem(tp + shift, n_tp),
        )
        for shift in range(1, n_tp)
    ]
    for copy in tp_copies:
        copy.start()

    def drain(i, carry):
        up_copy(i).wait_send()

        @pl.when(depth > 0)
        def _():
            down_copy(i).wait_send()

        side_copy(i).wait_send()
        core_copy(0, i).wait_send()
        core_copy(1, i).wait_send()
        return carry

    lax.fori_loop(0, chunks, drain, 0)
    for copy in [slope_side, slope_core, slope_on] + small_copies:
        copy.wait_send()
    for shift in range(1, n_tp):
        source = lax.rem(tp + n_tp - shift, n_tp)
        remote(
            tp_squares.at[source],
            tp_squares.at[source],
            tp_send.at[shift - 1],
            tp_recv.at[shift - 1],
            me,
            lax.rem(tp + shift, n_tp),
        ).wait_recv()
    for copy in tp_copies:
        copy.wait_send()
    everything = tp_squares[0]
    for other in range(1, n_tp):
        everything = everything + tp_squares[other]
    everything = jnp.sum(jnp.sum(everything, axis=0, keepdims=True), axis=1, keepdims=True)
    rescale_ref[...] = jnp.broadcast_to(
        lax.rsqrt(everything / scale_count + 1e-06), rescale_ref.shape
    )


def grad_sums(mesh, rows, slope, small, scale_count):
    n_ctx, n_tp = mesh.shape["ctx"], mesh.shape["tp"]
    positions, width = slope.shape
    chunks = rows.shape[2] // ROWS + 1
    dma = pltpu.SemaphoreType.DMA
    return pl.pallas_call(
        functools.partial(grad_kernel, n_ctx, n_tp, float(scale_count)),
        out_shape=(
            jax.ShapeDtypeStruct((QUADS, chunks, ROWS, width), jnp.bfloat16),
            jax.ShapeDtypeStruct((8, 128), jnp.float32),
        ),
        in_specs=[pl.BlockSpec(memory_space=pltpu.VMEM)] * 3,
        out_specs=(pl.BlockSpec(memory_space=pltpu.VMEM),) * 2,
        scratch_shapes=[
            pltpu.VMEM((3, positions, width), jnp.bfloat16),
            pltpu.VMEM((3, ROWS, width), jnp.bfloat16),
            pltpu.VMEM((chunks, ROWS, width), jnp.float32),
            pltpu.VMEM((chunks, ROWS, width), jnp.bfloat16),
            pltpu.VMEM((2, chunks, ROWS, width), jnp.bfloat16),
            pltpu.VMEM((QUADS, 8, width), jnp.float32),
            pltpu.VMEM((n_tp, 8, 128), jnp.float32),
            dma((3,)),
            dma((3,)),
            dma((3,)),
            dma((3,)),
            dma((chunks,)),
            dma((2, chunks)),
            dma((chunks,)),
            dma((chunks,)),
            dma((chunks,)),
            dma((chunks,)),
            dma((2, chunks)),
            dma((2, chunks)),
            dma((max(n_tp - 1, 1),)),
            dma((max(n_tp - 1, 1),)),
        ],
        compiler_params=pltpu.CompilerParams(
            collective_id=0, has_side_effects=True, vmem_limit_bytes=48 * 1024 * 1024
        ),
        cost_estimate=pl.CostEstimate(
            flops=2 * QUADS * positions * rows.shape[2] * width,
            bytes_accessed=4 * chunks * ROWS * width * 4,
            transcendentals=0,
        ),
    )(rows, slope, small)


def quarter_rows(mesh, gathered):
    n_ctx = mesh.shape["ctx"]
    quarter = gathered.shape[1] // QUADS
    quad = lax.rem(lax.axis_index("ctx"), QUADS)
    parts = []
    for m in range(QUADS):
        part = lax.dynamic_slice_in_dim(gathered, (quad ^ m) * quarter, quarter, 1)
        if m:
            part = lax.ppermute(part, "ctx", [(i, i ^ m) for i in range(n_ctx)])
        parts.append(part)
    return parts


def on_device(
    mesh,
    attended,
    out_proj,
    residual,
    norm_gain,
    cond_proj,
    noise_proj,
    latent_proj,
    noise_draws,
    targets,
):
    summed = lax.psum_scatter(
        jnp.dot(attended, out_proj, preferred_element_type=jnp.float32).astype(jnp.bfloat16),
        "tp",
        scatter_dimension=0,
        tiled=True,
    ).astype(jnp.float32)
    hidden = residual.astype(jnp.float32) + summed
    normed = (
        hidden * lax.rsqrt(jnp.mean(hidden * hidden, axis=-1, keepdims=True) + 1e-05) * norm_gain
    ).astype(jnp.bfloat16)
    gathered = lax.all_gather(normed, "tp", axis=0, tiled=True)
    near_rows = quarter_rows(mesh, gathered)
    condition = jnp.dot(gathered, cond_proj, preferred_element_type=jnp.float32)
    preact = condition[:, None, :] + jnp.einsum(
        "rsn,nh->rsh", noise_draws, noise_proj, preferred_element_type=jnp.float32
    )
    activation = jax.nn.silu(preact).astype(jnp.bfloat16)
    partial_samples = jnp.einsum(
        "rsh,hl->rsl", activation, latent_proj, preferred_element_type=jnp.float32
    )
    own_samples = lax.psum_scatter(partial_samples, "tp", scatter_dimension=0, tiled=True)
    energies, own_slopes = energy_score(own_samples, targets.astype(jnp.float32))
    slopes = lax.all_gather(own_slopes, "tp", axis=0, tiled=True)
    latent_part = jnp.einsum("rsh,rsl->lh", activation, slopes, preferred_element_type=jnp.float32)
    backward = jnp.einsum("rsl,hl->rsh", slopes, latent_proj, preferred_element_type=jnp.float32)
    pre_grad = (backward * silu_slope(preact)).astype(jnp.bfloat16)
    noise_part = jnp.einsum(
        "rsn,rsh->nh", noise_draws, pre_grad, preferred_element_type=jnp.float32
    )
    cond_slope = jnp.sum(pre_grad, axis=1, dtype=jnp.float32).astype(jnp.bfloat16)
    width = cond_slope.shape[1]
    small = jnp.concatenate([noise_part, latent_part], axis=0).astype(jnp.bfloat16)
    sums, rescale = grad_sums(
        mesh,
        jnp.stack(near_rows),
        cond_slope,
        small.reshape(QUADS, ROWS, width),
        D * HW + NZ * HW + HW * LAT,
    )
    rescale = rescale[0, 0]
    scaled = (sums.astype(jnp.float32) * rescale).astype(jnp.bfloat16)
    cond_out = scaled[:, :-1].reshape(D, width)
    small_out = scaled[:, -1].reshape(NZ + LAT, width)
    return (energies, cond_out, small_out[:NZ], small_out[NZ:].T)


def solution(mesh):
    return jax.shard_map(
        functools.partial(on_device, mesh),
        mesh=mesh,
        in_specs=(
            P("ctx", "tp"),
            P("tp", None),
            P(("ctx", "tp"), None),
            P(),
            P(None, "tp"),
            P(None, "tp"),
            P("tp", None),
            P("ctx", None, None),
            P(("ctx", "tp"), None),
        ),
        out_specs=(P(("ctx", "tp")), P(None, "tp"), P(None, "tp"), P("tp", None)),
        check_vma=False,
    )
```
